32 devices in a mesh: ind: 8 (over z, core), snp: 4 (over y, x).
Axes of the slice: x: 2, y: 2, z: 4, core: 2. Of those that a mesh axis runs over, the one named last changes fastest.
Arguments:
- dosages: int32 [2048, 2048], P(('snp', 'ind')), may hold values from 0 to 2
- allele_freq: float32 [2048], P(('snp', 'ind')), may hold values from 0.05 to 0.5
- earlier_factor: bfloat16 [2048, 8192], P(None, 'ind'), may hold values from -0.09375 to 0.09375
- earlier_solved: bfloat16 [8192, 2048], P('ind', 'snp'), may hold values from -6 to 6
- diag_inverse: bfloat16 [2048, 512], P('ind'), as said below
- update_products: bfloat16 [2048, 2048], P('ind'), may hold values from -0.125 to 0.125
Outputs:
- whitened: bfloat16 [2048, 2048], P('ind', 'snp')
The draws below stay inside these ranges and needn't reach their ends.
Inputs may be any that keep to these rules, and one draw needn't show every extreme that they name: `diag_inverse`: within each block of 512 rows the entry in row r and column c is zero where c > r mod 512; the entries with c = r mod 512 lie in 0.6 to 1.4.
All inputs are finite; a program needn't handle non-finite values.
Results may differ from the reference program's by a relative error of at most 0.0058.
Values may be sent and summed in bfloat16 or wider, within the bound.
A program may use at most 64 MiB of HBM per device.

```python
import math
import jax
import jax.numpy as jnp
from jax import lax

SLAB = 2048
BLK = 512
P_SIZE = 8192
S = 2048


def draw_dosages(key, part):
    level_key, first_key, second_key = jax.random.split(jax.random.fold_in(key, 11), 3)
    groups = 8
    levels = jax.random.randint(level_key, (S, groups), 5, 96)
    group_index = jnp.arange(SLAB) * groups // SLAB
    chosen = levels[:, group_index]
    allele_one = (jax.random.randint(first_key, (S, SLAB), 0, 100) < chosen).astype(jnp.int32)
    allele_two = (jax.random.randint(second_key, (S, SLAB), 0, 100) < chosen).astype(jnp.int32)
    return allele_one + allele_two


def draw_diag_inverse(key, part):
    normal_key, uniform_key = jax.random.split(jax.random.fold_in(key, 23))
    row_pos = jnp.arange(SLAB)[:, None] % BLK
    col_pos = jnp.arange(BLK)[None, :]
    below_diag = jax.random.normal(normal_key, (SLAB, BLK), jnp.float32) * (0.8 / math.sqrt(BLK))
    on_diag = jax.random.uniform(uniform_key, (SLAB, BLK), jnp.float32, 0.6, 1.4)
    values = jnp.where(col_pos < row_pos, below_diag, jnp.where(col_pos == row_pos, on_diag, 0.0))
    return values.astype(jnp.bfloat16)


def raised(values, own_key, source, target, blocks, factor):
    owner, partner = [(jnp.arange(values.shape[axis_at]) // (values.shape[axis_at] // blocks)).reshape([-1 if axis == axis_at else 1 for axis in range(values.ndim)]) for axis_at in (source, target)]
    chosen = jax.random.permutation(own_key, blocks)[partner]
    strong = (owner == chosen) | (owner == (partner + blocks // 2) % blocks)
    return jnp.where(strong, factor * values, values)


def block_levels(rng, shape, shards, smallest, high):
    def one(position, shards_of):
        steps = jax.random.uniform(jax.random.fold_in(jax.random.fold_in(rng, 6), position), (shards_of,), jnp.float32, smallest / len(shards), high / len(shards))
        return jnp.repeat(jnp.exp(steps), shape[position] // shards_of).reshape((-1,) + (1,) * (len(shape) - position - 1))

    level = one(*shards[0])
    for cut in shards[1:]:
        level = level * one(*cut)
    return level


def centred(stream_key, shape, deviation, bound, pieces=(), kind=jnp.bfloat16):
    level = block_levels(stream_key, shape, pieces, -0.22, 0.18) if pieces else 1.0
    entries = jax.random.normal(stream_key, shape, jnp.float32) * deviation * level
    return jnp.minimum(jnp.maximum(entries, -bound), bound).astype(kind)


def gaussian_with(key, dims, scale, most, cuts, heavy, dtype=jnp.bfloat16):
    drawn = scale * jax.random.normal(key, dims, jnp.float32)
    if cuts:
        drawn = drawn * block_levels(key, dims, cuts, -0.22, 0.18)
    return jnp.clip(raised(drawn, jax.random.fold_in(key, 3), *heavy), -most, most).astype(dtype)


def setup_inputs(seed: int = 0) -> dict:
    keys = jax.random.split(jax.random.key(seed), 7)
    return {
        "dosages": draw_dosages(jax.random.fold_in(keys[6], 71), 0),
        "allele_freq": jnp.clip(0.05 + 0.45 * jax.random.uniform(keys[1], (S,), jnp.float32) ** block_levels(keys[1], (S,), ((0, 32),), -0.2, 0.2), 0.05, 0.5),
        "earlier_factor": gaussian_with(keys[2], (SLAB, P_SIZE), P_SIZE ** -0.5, 0.09375, ((1, 8),), (1, 0, 8, 2.0)),
        "earlier_solved": centred(keys[3], (P_SIZE, S), 1.0, 6.0, ((0, 8), (1, 4))),
        "diag_inverse": draw_diag_inverse(jax.random.fold_in(keys[6], 71), 0),
        "update_products": centred(keys[5], (SLAB, SLAB), SLAB ** -0.5, 0.125, ((0, 8),)),
    }


def reference(dosages, allele_freq, earlier_factor, earlier_solved, diag_inverse, update_products):
    frequency = allele_freq[:, None]
    scaled = ((dosages.astype(jnp.float32) - 2.0 * frequency) * lax.rsqrt(2.0 * frequency * (1.0 - frequency))).astype(jnp.bfloat16)
    standardized = scaled.T
    update = jnp.dot(earlier_factor, earlier_solved, preferred_element_type=jnp.float32)
    residual = (standardized.astype(jnp.float32) - update).astype(jnp.bfloat16)
    blocks = SLAB // BLK
    solved = []
    for block in range(blocks):
        low_row = block * BLK
        diagonal_term = jnp.dot(diag_inverse[low_row:low_row + BLK], residual[low_row:low_row + BLK], preferred_element_type=jnp.float32)
        if block > 0:
            earlier_rows = jnp.concatenate(solved, 0)
            carried = jnp.dot(update_products[low_row:low_row + BLK, :low_row], earlier_rows, preferred_element_type=jnp.float32)
            diagonal_term = diagonal_term - carried
        solved.append(diagonal_term.astype(jnp.bfloat16))
    return jnp.concatenate(solved, 0)
```

```python
import functools
import jax
import jax.numpy as jnp
from jax import lax
from jax.experimental import pallas as pl
from jax.experimental.pallas import tpu as pltpu
from jax.sharding import PartitionSpec as P

BLK = 512
CW = 128
BF = jnp.bfloat16
F32 = jnp.float32


def fused(chips, dos_h, freq_ref, a_h, b_h, d_h, u_h, out_ref,
          dos, a, b, dfull, ufull, scaled, acc, sib_out, sib_in,
          up_out, up_in, dn_out, dn_in, w,
          ld_sem, a_sem, x_sem, sib_s, sib_r, up_s, up_r, dn_s, dn_r, w_s, w_r, o_s, o_r):
    me = lax.axis_index("ind")
    z, c = me // 2, me % 2
    sib = z * 2 + 1 - c
    half = b_h.shape[1] // 2
    chunks = half // CW
    rows = d_h.shape[0]
    ucols = ufull.shape[1]
    snps = dos_h.shape[0]

    def remote(src, dst, ss, rs, to):
        return pltpu.make_async_remote_copy(
            src_ref=src, dst_ref=dst, send_sem=ss, recv_sem=rs,
            device_id={"ind": to}, device_id_type=pl.DeviceIdType.MESH)

    last = chips - 1

    def block_at(j):
        bottom = jnp.where(j < last - 1, j + 2, last - j)
        return jnp.where(z == 0, bottom, lax.rem(z + 1 + j, chips))

    def load_a(j):
        at = pl.ds(pl.multiple_of(block_at(j) * BLK, BLK), BLK)
        return pltpu.make_async_copy(a_h.at[at], a.at[at], a_sem.at[j])

    my_rows = pl.ds(pl.multiple_of(c * rows, rows), rows)
    load_dos = pltpu.make_async_copy(dos_h, dos, ld_sem.at[0])
    load_b = pltpu.make_async_copy(b_h, b, ld_sem.at[1])
    load_d = pltpu.make_async_copy(d_h, dfull.at[my_rows], ld_sem.at[2])
    load_u = pltpu.make_async_copy(u_h.at[:, :ucols], ufull.at[my_rows], ld_sem.at[3])
    load_dos.start()
    load_b.start()
    for j in range(chips):
        load_a(j).start()
    load_d.start()
    load_u.start()

    barrier = pltpu.get_barrier_semaphore()

    def greet(to):
        pl.semaphore_signal(barrier, inc=1, device_id={"ind": to},
                            device_id_type=pl.DeviceIdType.MESH)

    greet(sib)

    @pl.when(z > 0)
    def _():
        greet(me - 2)

    @pl.when(z < chips - 1)
    def _():
        greet(me + 2)

    load_dos.wait()
    frow = freq_ref[...]
    eye = (lax.broadcasted_iota(jnp.int32, (snps, snps), 0)
           == lax.broadcasted_iota(jnp.int32, (snps, snps), 1))
    freq = jnp.sum(jnp.where(eye, jnp.broadcast_to(frow, (snps, snps)), 0.0), axis=1, keepdims=True)
    scaled[...] = ((dos[...].astype(F32) - 2.0 * freq)
                   * lax.rsqrt(2.0 * freq * (1.0 - freq))).astype(BF)

    @pl.when((z == 0) | (z == chips - 1))
    def _():
        pl.semaphore_wait(barrier, 2)

    @pl.when((z > 0) & (z < chips - 1))
    def _():
        pl.semaphore_wait(barrier, 3)

    xd = remote(d_h, dfull.at[my_rows], x_sem.at[0], x_sem.at[1], sib)
    xu = remote(u_h.at[:, :ucols], ufull.at[my_rows], x_sem.at[2], x_sem.at[3], sib)

    def sib_copy(blk):
        return remote(sib_out.at[blk], sib_in.at[blk], sib_s.at[blk], sib_r.at[blk], sib)

    def up_copy(blk, q):
        return remote(up_out.at[blk, q], up_in.at[blk, q], up_s.at[blk, q], up_r.at[blk, q], me + 2)

    def dn_copy(blk, q):
        return remote(dn_out.at[blk, q], dn_in.at[blk, q], dn_s.at[blk, q], dn_r.at[blk, q], me - 2)

    def w_copy(blk, q):
        return remote(w.at[blk, q], w.at[blk, q], w_s.at[blk, q], w_r.at[blk, q], me + 2)

    def out_copy(q):
        return remote(
            w.at[z, q, pl.ds(pl.multiple_of((1 - c) * rows, rows), rows)],
            out_ref.at[:, pl.ds(pl.multiple_of(c * half + q * CW, CW), CW)],
            o_s.at[q], o_r.at[q], sib)

    def partial(blk, side):
        at = pl.ds(pl.multiple_of(blk * BLK, BLK), BLK)
        cols = pl.ds(pl.multiple_of(side * half, half), half)
        place = (lax.broadcasted_iota(jnp.int32, (snps, half), 1) + side * half
                 == lax.broadcasted_iota(jnp.int32, (snps, half), 0) + me * snps)
        own = lax.dot_general(scaled[:, at], place.astype(F32).astype(BF),
                              (((0,), (0,)), ((), ())), preferred_element_type=F32)
        return own - jnp.dot(a[at, :], b[:, cols], preferred_element_type=F32)

    def finish(blk):
        sib_copy(blk).wait_recv()
        for q in range(chunks):
            total = acc[blk, q] + sib_in[blk, :, q * CW:(q + 1) * CW].astype(F32)
            acc[blk, q] = total

            @pl.when((z == 0) & (blk > 0))
            def _():
                up_out[blk, q] = total.astype(BF)

            @pl.when((z == 0) & (blk > (1 if q else 0)))
            def _():
                up_copy(blk, q).start()

            @pl.when((z == chips - 1) & (blk < chips - 1))
            def _():
                dn_out[blk, q] = total.astype(BF)
                dn_copy(blk, q).start()

    load_b.wait()

    def step(j, carry):
        load_a(j).wait()
        blk = block_at(j)
        sib_out[blk] = partial(blk, 1 - c).astype(BF)
        sib_copy(blk).start()
        own = partial(blk, c)
        for q in range(chunks):
            acc[blk, q] = own[:, q * CW:(q + 1) * CW]

        @pl.when(j > 0)
        def _():
            finish(block_at(j - 1))

        return carry

    lax.fori_loop(0, chips, step, 0)
    xd.start()
    xu.start()
    finish(block_at(chips - 1))

    def role(zz):
        sent = []

        def send(copy):
            copy.start()
            sent.append(copy)

        def relay_up(blk, q):
            up_copy(blk, q).wait_recv()
            up_out[blk, q] = (acc[blk, q] + up_in[blk, q].astype(F32)).astype(BF)
            send(up_copy(blk, q))

        def relay_dn(blk, q):
            dn_copy(blk, q).wait_recv()
            dn_out[blk, q] = (acc[blk, q] + dn_in[blk, q].astype(F32)).astype(BF)
            send(dn_copy(blk, q))

        def residual(q):
            total = acc[zz, q]
            if zz < last:
                dn_copy(zz, q).wait_recv()
                total = total + dn_in[zz, q].astype(F32)
            if zz > 0:
                up_copy(zz, q).wait_recv()
                total = total + up_in[zz, q].astype(F32)
            acc[zz, q] = jnp.dot(dfull[...], total.astype(BF), preferred_element_type=F32)

        ready = []

        def weights():
            if not ready:
                load_d.wait()
                load_u.wait()
                xd.wait_recv()
                xu.wait_recv()
                ready.append(1)

        if 0 < zz < last:
            pieces = [(last - zz + k, q, 0, k) for k in range(zz) for q in range(chunks)]
            pieces += [(zz + k - 2, q, 1, k) for k in range(zz + 1, chips) for q in range(chunks)]
            for _, q, up, k in sorted(pieces):
                (relay_up if up else relay_dn)(k, q)
        weights()
        for q in range(chunks):
            residual(q)
            for k in range(zz):
                w_copy(k, q).wait_recv()
                if zz < last:
                    send(w_copy(k, q))
                acc[zz, q] = acc[zz, q] - jnp.dot(
                    ufull[:, k * BLK:(k + 1) * BLK], w[k, q], preferred_element_type=F32)
            finish_chunk(zz, q, send)
            if zz == 0 and q + 1 < chunks:
                up_copy(1, q + 1).start()
        for copy in sent:
            copy.wait_send()
        if zz == 0:
            for k in range(1, chips):
                for q in range(chunks):
                    up_copy(k, q).wait_send()
        if zz == last:
            for k in range(last):
                for q in range(chunks):
                    dn_copy(k, q).wait_send()

    def finish_chunk(zz, q, send):
        w[zz, q] = acc[zz, q].astype(BF)
        if zz < chips - 1:
            send(w_copy(zz, q))
        send(out_copy(q))
        out_ref[:, pl.ds(pl.multiple_of(c * half + q * CW, CW), CW)] = w[zz, q, my_rows, :]

    for zz in range(chips):
        pl.when(z == zz)(functools.partial(role, zz))

    for q in range(chunks):
        out_copy(q).wait_recv()
    for k in range(chips):
        sib_copy(k).wait_send()
    xd.wait_send()
    xu.wait_send()


def fused_call(dosages, allele_freq, earlier_factor, earlier_solved, diag_inverse, update_products):
    slab = earlier_factor.shape[0]
    chips = slab // BLK
    snps = dosages.shape[0]
    width = earlier_solved.shape[1]
    half = width // 2
    chunks = half // CW
    rows = diag_inverse.shape[0]
    depth = earlier_factor.shape[1]
    pieces = (chips, chunks, BLK, CW)
    dma = pltpu.SemaphoreType.DMA
    hbm = pl.BlockSpec(memory_space=pl.ANY)
    vmem = pl.BlockSpec(memory_space=pltpu.VMEM)
    macs = slab * depth * width + rows * (BLK + slab) * width
    return pl.pallas_call(
        functools.partial(fused, chips),
        out_shape=jax.ShapeDtypeStruct((rows, width), BF),
        in_specs=[hbm, vmem, hbm, hbm, hbm, hbm],
        out_specs=vmem,
        scratch_shapes=[
            pltpu.VMEM((snps, slab), jnp.int32),
            pltpu.VMEM((slab, depth), BF),
            pltpu.VMEM((depth, width), BF),
            pltpu.VMEM((BLK, BLK), BF),
            pltpu.VMEM((BLK, slab - BLK), BF),
            pltpu.VMEM((snps, slab), BF),
            pltpu.VMEM(pieces, F32),
            pltpu.VMEM((chips, BLK, half), BF),
            pltpu.VMEM((chips, BLK, half), BF),
            pltpu.VMEM(pieces, BF),
            pltpu.VMEM(pieces, BF),
            pltpu.VMEM(pieces, BF),
            pltpu.VMEM(pieces, BF),
            pltpu.VMEM(pieces, BF),
            dma((4,)), dma((chips,)), dma((4,)), dma((chips,)), dma((chips,)),
            dma((chips, chunks)), dma((chips, chunks)),
            dma((chips, chunks)), dma((chips, chunks)),
            dma((chips, chunks)), dma((chips, chunks)),
            dma((chunks,)), dma((chunks,)),
        ],
        compiler_params=pltpu.CompilerParams(
            collective_id=0, has_side_effects=True, vmem_limit_bytes=60 * 2**20),
        cost_estimate=pl.CostEstimate(
            flops=2 * macs, bytes_accessed=8 * 2**20, transcendentals=0),
    )(dosages, allele_freq.reshape(1, snps), earlier_factor, earlier_solved,
      diag_inverse, update_products)


def exchange_2(value, axis, stride):
    mask = 2**stride
    pairs = [(source, source ^ mask) for source in range(lax.axis_size(axis))]
    return lax.ppermute(value, axis, pairs)


def general(dosages, allele_freq, earlier_factor, earlier_solved, diag_inverse, update_products):
    slab = earlier_factor.shape[0]
    frequency = allele_freq[:, None]
    scaled = (
        (dosages.astype(F32) - 2.0 * frequency)
        * lax.rsqrt(2.0 * frequency * (1.0 - frequency))
    ).astype(BF)
    arrived = lax.all_to_all(scaled, "ind", split_axis=1, concat_axis=0, tiled=True)
    rows_dev = diag_inverse.shape[0]
    update = lax.psum_scatter(
        jnp.dot(earlier_factor, earlier_solved, preferred_element_type=F32),
        "ind", scatter_dimension=0, tiled=True)
    residual = (arrived.T.astype(F32) - update).astype(BF)
    position = lax.axis_index("ind")
    my_block = position * rows_dev // BLK
    held = residual
    for bit in range((BLK // rows_dev).bit_length() - 1):
        other = exchange_2(held, "ind", bit)
        held = jnp.where(
            position // 2**bit % 2 == 0,
            jnp.concatenate((held, other), 0), jnp.concatenate((other, held), 0))
    diagonal_term = jnp.dot(diag_inverse, held, preferred_element_type=F32)
    solved = jnp.where(my_block == 0, diagonal_term.astype(BF), jnp.zeros_like(residual))
    for block in range(1, slab // BLK):
        carried = jnp.dot(
            update_products, lax.all_gather(solved, "ind", axis=0, tiled=True),
            preferred_element_type=F32)
        solved = jnp.where(my_block == block, (diagonal_term - carried).astype(BF), solved)
    return solved


def solution(mesh):
    def per_device(*args):
        slab = args[2].shape[0]
        if mesh.shape["ind"] * BLK == 2 * slab and args[3].shape[1] % (2 * CW) == 0:
            return fused_call(*args)
        return general(*args)

    placed = (
        P(("snp", "ind"), None),
        P(("snp", "ind")),
        P(None, "ind"),
        P("ind", "snp"),
        P("ind", None),
        P("ind", None),
    )
    return jax.shard_map(
        per_device, mesh=mesh, in_specs=placed, out_specs=P("ind", "snp"), check_vma=False
    )
```

```python
import functools
import jax
import jax.numpy as jnp
from jax import lax
from jax.experimental import pallas as pl
from jax.experimental.pallas import tpu as pltpu
from jax.sharding import PartitionSpec as P

BLK = 512
CW = 128
PR = 256
PARTS = BLK // PR
BF = jnp.bfloat16
F32 = jnp.float32


def fused(chips, dos_h, freq_ref, a_h, b_h, d_h, u_h, out_ref,
          dos, a, b, dfull, ufull, scaled, acc, sib_out, sib_in,
          up_out, up_in, dn_out, dn_in, w,
          ld_sem, a_sem, x_sem, sib_s, sib_r, up_s, up_r, dn_s, dn_r, w_s, w_r, o_s, o_r):
    me = lax.axis_index("ind")
    z, c = me // 2, me % 2
    sib = z * 2 + 1 - c
    half = b_h.shape[1] // 2
    chunks = half // CW
    rows = d_h.shape[0]
    ucols = ufull.shape[1]
    snps = dos_h.shape[0]

    def remote(src, dst, ss, rs, to):
        return pltpu.make_async_remote_copy(
            src_ref=src, dst_ref=dst, send_sem=ss, recv_sem=rs,
            device_id={"ind": to}, device_id_type=pl.DeviceIdType.MESH)

    last = chips - 1

    def block_at(j):
        bottom = jnp.where(j == 0, last, jnp.where(j == last, 0, j))
        return jnp.where(z == 0, bottom, lax.rem(z + 1 + j, chips))

    def load_a(j):
        at = pl.ds(pl.multiple_of(block_at(j) * BLK, BLK), BLK)
        return pltpu.make_async_copy(a_h.at[at], a.at[at], a_sem.at[j])

    my_rows = pl.ds(pl.multiple_of(c * rows, rows), rows)
    load_dos = pltpu.make_async_copy(dos_h, dos, ld_sem.at[0])
    load_b = pltpu.make_async_copy(b_h, b, ld_sem.at[1])
    load_d = pltpu.make_async_copy(d_h, dfull.at[my_rows], ld_sem.at[2])
    load_u = pltpu.make_async_copy(u_h.at[:, :ucols], ufull.at[my_rows], ld_sem.at[3])
    load_dos.start()
    load_b.start()
    for j in range(chips):
        load_a(j).start()
    load_d.start()
    load_u.start()

    barrier = pltpu.get_barrier_semaphore()

    def greet(to):
        pl.semaphore_signal(barrier, inc=1, device_id={"ind": to},
                            device_id_type=pl.DeviceIdType.MESH)

    greet(sib)

    @pl.when(z > 0)
    def _():
        greet(me - 2)

    @pl.when(z < chips - 1)
    def _():
        greet(me + 2)

    load_dos.wait()
    frow = freq_ref[...]
    eye = (lax.broadcasted_iota(jnp.int32, (snps, snps), 0)
           == lax.broadcasted_iota(jnp.int32, (snps, snps), 1))
    freq = jnp.sum(jnp.where(eye, jnp.broadcast_to(frow, (snps, snps)), 0.0), axis=1, keepdims=True)
    scaled[...] = ((dos[...].astype(F32) - 2.0 * freq)
                   * lax.rsqrt(2.0 * freq * (1.0 - freq))).astype(BF)

    @pl.when((z == 0) | (z == chips - 1))
    def _():
        pl.semaphore_wait(barrier, 2)

    @pl.when((z > 0) & (z < chips - 1))
    def _():
        pl.semaphore_wait(barrier, 3)

    xd = remote(d_h, dfull.at[my_rows], x_sem.at[0], x_sem.at[1], sib)
    xu = remote(u_h.at[:, :ucols], ufull.at[my_rows], x_sem.at[2], x_sem.at[3], sib)

    def sib_copy(blk):
        return remote(sib_out.at[blk], sib_in.at[blk], sib_s.at[blk], sib_r.at[blk], sib)

    def piece(buf, blk, q, h):
        return buf.at[blk, q, pl.ds(h * PR, PR)]

    def line_copy(src, dst, ss, rs, blk, q, h, to):
        return remote(piece(src, blk, q, h), piece(dst, blk, q, h),
                      ss.at[blk, q * PARTS + h], rs.at[blk, q * PARTS + h], to)

    def up_copy(blk, q, h):
        return line_copy(up_out, up_in, up_s, up_r, blk, q, h, me + 2)

    def dn_copy(blk, q, h):
        return line_copy(dn_out, dn_in, dn_s, dn_r, blk, q, h, me - 2)

    def w_copy(blk, q, h):
        return line_copy(w, w, w_s, w_r, blk, q, h, me + 2)

    def out_copy(q):
        return remote(
            w.at[z, q, pl.ds(pl.multiple_of((1 - c) * rows, rows), rows)],
            out_ref.at[:, pl.ds(pl.multiple_of(c * half + q * CW, CW), CW)],
            o_s.at[q], o_r.at[q], sib)

    def partial(blk, side):
        at = pl.ds(pl.multiple_of(blk * BLK, BLK), BLK)
        cols = pl.ds(pl.multiple_of(side * half, half), half)
        place = (lax.broadcasted_iota(jnp.int32, (snps, half), 1) + side * half
                 == lax.broadcasted_iota(jnp.int32, (snps, half), 0) + me * snps)
        own = lax.dot_general(scaled[:, at], place.astype(F32).astype(BF),
                              (((0,), (0,)), ((), ())), preferred_element_type=F32)
        return own - jnp.dot(a[at, :], b[:, cols], preferred_element_type=F32)

    def finish(blk):
        sib_copy(blk).wait_recv()
        for q in range(chunks):
            total = acc[blk, q] + sib_in[blk, :, q * CW:(q + 1) * CW].astype(F32)
            acc[blk, q] = total

            @pl.when((z == 0) & (blk > 0))
            def _():
                up_out[blk, q] = total.astype(BF)

            @pl.when((z == 0) & (blk > (last - 1 if q else 0)))
            def _():
                for h in range(PARTS):
                    up_copy(blk, q, h).start()

            @pl.when((z == last) & (blk < last))
            def _():
                dn_out[blk, q] = total.astype(BF)
                for h in range(PARTS):
                    dn_copy(blk, q, h).start()

    load_b.wait()

    def step(j, carry):
        load_a(j).wait()
        blk = block_at(j)
        sib_out[blk] = partial(blk, 1 - c).astype(BF)
        sib_copy(blk).start()
        own = partial(blk, c)
        for q in range(chunks):
            acc[blk, q] = own[:, q * CW:(q + 1) * CW]

        @pl.when(j > 0)
        def _():
            finish(block_at(j - 1))

        return carry

    lax.fori_loop(0, chips, step, 0)
    xd.start()
    xu.start()
    finish(block_at(chips - 1))

    def role(zz):
        sent = []

        def send(copy):
            copy.start()
            sent.append(copy)

        def relay(copy, out, arrived, blk, q):
            for h in range(PARTS):
                at = slice(h * PR, (h + 1) * PR)
                copy(blk, q, h).wait_recv()
                out[blk, q, at] = (acc[blk, q, at] + arrived[blk, q, at].astype(F32)).astype(BF)
                send(copy(blk, q, h))

        def relay_up(blk, q):
            relay(up_copy, up_out, up_in, blk, q)

        def relay_dn(blk, q):
            relay(dn_copy, dn_out, dn_in, blk, q)

        def residual(q):
            total = acc[zz, q]
            if zz < last:
                for h in range(PARTS):
                    dn_copy(zz, q, h).wait_recv()
                total = total + dn_in[zz, q].astype(F32)
            if zz > 0:
                for h in range(PARTS):
                    up_copy(zz, q, h).wait_recv()
                total = total + up_in[zz, q].astype(F32)
            acc[zz, q] = jnp.dot(dfull[...], total.astype(BF), preferred_element_type=F32)

        ready = []

        def weights():
            if not ready:
                load_d.wait()
                load_u.wait()
                xd.wait_recv()
                xu.wait_recv()
                ready.append(1)

        if 0 < zz < last:
            pieces = [(2 * k + last - zz + q + 0.5, q, 0, k) for k in range(zz) for q in range(chunks)]
            pieces += [(zz + q, q, 1, last) for q in range(chunks)]
            pieces += [(zz + 1 + k, 0, 1, k) for k in range(zz + 1, last)]
            for _, q, up, k in sorted(pieces):
                (relay_up if up else relay_dn)(k, q)
        weights()
        for q in range(chunks):
            if q:
                for k in range(zz + 1, last):
                    if zz > 0:
                        relay_up(k, q)
            residual(q)
            for k in range(zz):
                for h in range(PARTS):
                    w_copy(k, q, h).wait_recv()
                    if zz < last:
                        send(w_copy(k, q, h))
                acc[zz, q] = acc[zz, q] - jnp.dot(
                    ufull[:, k * BLK:(k + 1) * BLK], w[k, q], preferred_element_type=F32)
            w[zz, q] = acc[zz, q].astype(BF)
            if zz < last:
                for h in range(PARTS):
                    send(w_copy(zz, q, h))
            send(out_copy(q))
            out_ref[:, pl.ds(pl.multiple_of(c * half + q * CW, CW), CW)] = w[zz, q, my_rows, :]
            if zz == 0 and q + 1 < chunks:
                for k in range(1, last):
                    for h in range(PARTS):
                        up_copy(k, q + 1, h).start()
        for copy in sent:
            copy.wait_send()
        for q in range(chunks):
            for h in range(PARTS):
                if zz == 0:
                    for k in range(1, chips):
                        up_copy(k, q, h).wait_send()
                if zz == last:
                    for k in range(last):
                        dn_copy(k, q, h).wait_send()

    for zz in range(chips):
        pl.when(z == zz)(functools.partial(role, zz))

    for q in range(chunks):
        out_copy(q).wait_recv()
    for k in range(chips):
        sib_copy(k).wait_send()
    xd.wait_send()
    xu.wait_send()


def fused_call(dosages, allele_freq, earlier_factor, earlier_solved, diag_inverse, update_products):
    slab = earlier_factor.shape[0]
    chips = slab // BLK
    snps = dosages.shape[0]
    width = earlier_solved.shape[1]
    half = width // 2
    chunks = half // CW
    rows = diag_inverse.shape[0]
    depth = earlier_factor.shape[1]
    pieces = (chips, chunks, BLK, CW)
    dma = pltpu.SemaphoreType.DMA
    hbm = pl.BlockSpec(memory_space=pl.ANY)
    vmem = pl.BlockSpec(memory_space=pltpu.VMEM)
    macs = slab * depth * width + rows * (BLK + slab) * width
    return pl.pallas_call(
        functools.partial(fused, chips),
        out_shape=jax.ShapeDtypeStruct((rows, width), BF),
        in_specs=[hbm, vmem, hbm, hbm, hbm, hbm],
        out_specs=vmem,
        scratch_shapes=[
            pltpu.VMEM((snps, slab), jnp.int32),
            pltpu.VMEM((slab, depth), BF),
            pltpu.VMEM((depth, width), BF),
            pltpu.VMEM((BLK, BLK), BF),
            pltpu.VMEM((BLK, slab - BLK), BF),
            pltpu.VMEM((snps, slab), BF),
            pltpu.VMEM(pieces, F32),
            pltpu.VMEM((chips, BLK, half), BF),
            pltpu.VMEM((chips, BLK, half), BF),
            pltpu.VMEM(pieces, BF),
            pltpu.VMEM(pieces, BF),
            pltpu.VMEM(pieces, BF),
            pltpu.VMEM(pieces, BF),
            pltpu.VMEM(pieces, BF),
            dma((4,)), dma((chips,)), dma((4,)), dma((chips,)), dma((chips,)),
            *[dma((chips, chunks * PARTS))] * 6,
            dma((chunks,)), dma((chunks,)),
        ],
        compiler_params=pltpu.CompilerParams(
            collective_id=0, has_side_effects=True, vmem_limit_bytes=60 * 2**20),
        cost_estimate=pl.CostEstimate(
            flops=2 * macs, bytes_accessed=8 * 2**20, transcendentals=0),
    )(dosages, allele_freq.reshape(1, snps), earlier_factor, earlier_solved,
      diag_inverse, update_products)


def exchange_2(value, axis, stride):
    mask = 2**stride
    pairs = [(source, source ^ mask) for source in range(lax.axis_size(axis))]
    return lax.ppermute(value, axis, pairs)


def general(dosages, allele_freq, earlier_factor, earlier_solved, diag_inverse, update_products):
    slab = earlier_factor.shape[0]
    frequency = allele_freq[:, None]
    scaled = (
        (dosages.astype(F32) - 2.0 * frequency)
        * lax.rsqrt(2.0 * frequency * (1.0 - frequency))
    ).astype(BF)
    arrived = lax.all_to_all(scaled, "ind", split_axis=1, concat_axis=0, tiled=True)
    rows_dev = diag_inverse.shape[0]
    update = lax.psum_scatter(
        jnp.dot(earlier_factor, earlier_solved, preferred_element_type=F32),
        "ind", scatter_dimension=0, tiled=True)
    residual = (arrived.T.astype(F32) - update).astype(BF)
    position = lax.axis_index("ind")
    my_block = position * rows_dev // BLK
    held = residual
    for bit in range((BLK // rows_dev).bit_length() - 1):
        other = exchange_2(held, "ind", bit)
        held = jnp.where(
            position // 2**bit % 2 == 0,
            jnp.concatenate((held, other), 0), jnp.concatenate((other, held), 0))
    diagonal_term = jnp.dot(diag_inverse, held, preferred_element_type=F32)
    solved = jnp.where(my_block == 0, diagonal_term.astype(BF), jnp.zeros_like(residual))
    for block in range(1, slab // BLK):
        carried = jnp.dot(
            update_products, lax.all_gather(solved, "ind", axis=0, tiled=True),
            preferred_element_type=F32)
        solved = jnp.where(my_block == block, (diagonal_term - carried).astype(BF), solved)
    return solved


def solution(mesh):
    def per_device(*args):
        slab = args[2].shape[0]
        if mesh.shape["ind"] * BLK == 2 * slab and args[3].shape[1] % (2 * CW) == 0:
            return fused_call(*args)
        return general(*args)

    placed = (
        P(("snp", "ind"), None),
        P(("snp", "ind")),
        P(None, "ind"),
        P("ind", "snp"),
        P("ind", None),
        P("ind", None),
    )
    return jax.shard_map(
        per_device, mesh=mesh, in_specs=placed, out_specs=P("ind", "snp"), check_vma=False
    )
```

```python
import functools
import jax
import jax.numpy as jnp
from jax import lax
from jax.experimental import pallas as pl
from jax.experimental.pallas import tpu as pltpu
from jax.sharding import PartitionSpec as P

BLK = 512
CW = 128
PR = 256
PARTS = BLK // PR
BF = jnp.bfloat16
F32 = jnp.float32


def fused(chips, dos_h, freq_ref, a_h, b_h, d_h, u_h, out_ref,
          dos, a, b, dfull, ufull, placed, acc, sib_out, sib_in,
          up_out, up_in, dn_out, dn_in, w,
          ld_sem, a_sem, x_sem, sib_s, sib_r, up_s, up_r, dn_s, dn_r, w_s, w_r, o_s, o_r, l_s):
    me = lax.axis_index("ind")
    z, c = me // 2, me % 2
    sib = z * 2 + 1 - c
    half = b_h.shape[1] // 2
    chunks = half // CW
    rows = d_h.shape[0]
    ucols = ufull.shape[1]
    snps = dos_h.shape[0]

    def remote(src, dst, ss, rs, to):
        return pltpu.make_async_remote_copy(
            src_ref=src, dst_ref=dst, send_sem=ss, recv_sem=rs,
            device_id={"ind": to}, device_id_type=pl.DeviceIdType.MESH)

    last = chips - 1

    def block_at(j):
        bottom = jnp.where(j == 0, last, jnp.where(j == last, 0, j))
        return jnp.where(z == 0, bottom, lax.rem(z + 1 + j, chips))

    def load_a(j):
        at = pl.ds(pl.multiple_of(block_at(j) * BLK, BLK), BLK)
        return pltpu.make_async_copy(a_h.at[at], a.at[at], a_sem.at[j])

    my_rows = pl.ds(pl.multiple_of(c * rows, rows), rows)
    load_dos = pltpu.make_async_copy(dos_h, dos, ld_sem.at[0])
    load_b = pltpu.make_async_copy(b_h, b, ld_sem.at[1])
    load_d = pltpu.make_async_copy(d_h, dfull.at[my_rows], ld_sem.at[2])
    load_u = pltpu.make_async_copy(u_h.at[:, :ucols], ufull.at[my_rows], ld_sem.at[3])
    load_dos.start()
    load_b.start()
    for j in range(chips):
        load_a(j).start()
    load_d.start()
    load_u.start()

    barrier = pltpu.get_barrier_semaphore()

    def greet(to):
        pl.semaphore_signal(barrier, inc=1, device_id={"ind": to},
                            device_id_type=pl.DeviceIdType.MESH)

    greet(sib)

    @pl.when(z > 0)
    def _():
        greet(me - 2)

    @pl.when(z < chips - 1)
    def _():
        greet(me + 2)

    load_dos.wait()
    frow = freq_ref[...]
    eye = (lax.broadcasted_iota(jnp.int32, (snps, snps), 0)
           == lax.broadcasted_iota(jnp.int32, (snps, snps), 1))
    freq = jnp.sum(jnp.where(eye, jnp.broadcast_to(frow, (snps, snps)), 0.0), axis=1, keepdims=True)
    scaled = ((dos[...].astype(F32) - 2.0 * freq)
              * lax.rsqrt(2.0 * freq * (1.0 - freq))).astype(BF)
    my_side = me * snps // half
    place = (lax.broadcasted_iota(jnp.int32, (snps, half), 1) + my_side * half
             == lax.broadcasted_iota(jnp.int32, (snps, half), 0) + me * snps)
    placed[...] = lax.dot_general(scaled, place.astype(F32).astype(BF), (((0,), (0,)), ((), ())),
                                  preferred_element_type=F32).astype(BF)

    @pl.when((z == 0) | (z == chips - 1))
    def _():
        pl.semaphore_wait(barrier, 2)

    @pl.when((z > 0) & (z < chips - 1))
    def _():
        pl.semaphore_wait(barrier, 3)

    xd = remote(d_h, dfull.at[my_rows], x_sem.at[0], x_sem.at[1], sib)
    xu = remote(u_h.at[:, :ucols], ufull.at[my_rows], x_sem.at[2], x_sem.at[3], sib)

    def sib_copy(blk):
        return remote(sib_out.at[blk], sib_in.at[blk], sib_s.at[blk], sib_r.at[blk], sib)

    def piece(buf, blk, q, h):
        return buf.at[blk, q, pl.ds(h * PR, PR)]

    def line_copy(src, dst, ss, rs, blk, q, h, to):
        return remote(piece(src, blk, q, h), piece(dst, blk, q, h),
                      ss.at[blk, q * PARTS + h], rs.at[blk, q * PARTS + h], to)

    def up_copy(blk, q, h):
        return line_copy(up_out, up_in, up_s, up_r, blk, q, h, me + 2)

    def dn_copy(blk, q, h):
        return line_copy(dn_out, dn_in, dn_s, dn_r, blk, q, h, me - 2)

    def w_copy(blk, q, h):
        return line_copy(w, w, w_s, w_r, blk, q, h, me + 2)

    def out_copy(q):
        return remote(
            w.at[z, q, pl.ds(pl.multiple_of((1 - c) * rows, rows), rows)],
            out_ref.at[:, pl.ds(pl.multiple_of(c * half + q * CW, CW), CW)],
            o_s.at[q], o_r.at[q], sib)

    def own_copy(q):
        return pltpu.make_async_copy(
            w.at[z, q, my_rows],
            out_ref.at[:, pl.ds(pl.multiple_of(c * half + q * CW, CW), CW)], l_s.at[q])

    def partial(blk, side):
        at = pl.ds(pl.multiple_of(blk * BLK, BLK), BLK)
        cols = pl.ds(pl.multiple_of(side * half, half), half)
        own = jnp.where(side == my_side, placed[at, :].astype(F32), 0.0)
        return own - jnp.dot(a[at, :], b[:, cols], preferred_element_type=F32)

    def finish(blk):
        sib_copy(blk).wait_recv()
        for q in range(chunks):
            total = acc[blk, q] + sib_in[blk, :, q * CW:(q + 1) * CW].astype(F32)
            acc[blk, q] = total

            @pl.when((z == 0) & (blk > 0))
            def _():
                up_out[blk, q] = total.astype(BF)

            @pl.when((z == 0) & (blk > (last - 1 if q else 0)))
            def _():
                for h in range(PARTS):
                    up_copy(blk, q, h).start()

            @pl.when((z == last) & (blk < last))
            def _():
                dn_out[blk, q] = total.astype(BF)
                for h in range(PARTS):
                    dn_copy(blk, q, h).start()

    load_b.wait()

    def step(j, carry):
        load_a(j).wait()
        blk = block_at(j)
        sib_out[blk] = partial(blk, 1 - c).astype(BF)
        sib_copy(blk).start()
        own = partial(blk, c)
        for q in range(chunks):
            acc[blk, q] = own[:, q * CW:(q + 1) * CW]

        @pl.when(j > 0)
        def _():
            finish(block_at(j - 1))

        return carry

    lax.fori_loop(0, chips, step, 0)
    xd.start()
    xu.start()
    finish(block_at(chips - 1))

    def role(zz):
        sent = []

        def send(copy):
            copy.start()
            sent.append(copy)

        def relay(copy, out, arrived, blk, q):
            for h in range(PARTS):
                at = slice(h * PR, (h + 1) * PR)
                copy(blk, q, h).wait_recv()
                out[blk, q, at] = (acc[blk, q, at] + arrived[blk, q, at].astype(F32)).astype(BF)
                send(copy(blk, q, h))

        def relay_up(blk, q):
            relay(up_copy, up_out, up_in, blk, q)

        def relay_dn(blk, q):
            relay(dn_copy, dn_out, dn_in, blk, q)

        def residual(q):
            total = acc[zz, q]
            if zz < last:
                for h in range(PARTS):
                    dn_copy(zz, q, h).wait_recv()
                total = total + dn_in[zz, q].astype(F32)
            if zz > 0:
                for h in range(PARTS):
                    up_copy(zz, q, h).wait_recv()
                total = total + up_in[zz, q].astype(F32)
            acc[zz, q] = jnp.dot(dfull[...], total.astype(BF), preferred_element_type=F32)

        ready = []

        def weights():
            if not ready:
                load_d.wait()
                load_u.wait()
                xd.wait_recv()
                xu.wait_recv()
                ready.append(1)

        if 0 < zz < last:
            pieces = [(2 * k + last - zz + q + 0.5, q, 0, k) for k in range(zz) for q in range(chunks)]
            pieces += [(zz + q, q, 1, last) for q in range(chunks)]
            pieces += [(zz + 1 + k, 0, 1, k) for k in range(zz + 1, last)]
            for _, q, up, k in sorted(pieces):
                (relay_up if up else relay_dn)(k, q)
        weights()
        for q in range(chunks):
            if q:
                for k in range(zz + 1, last):
                    if zz > 0:
                        relay_up(k, q)
            residual(q)
            for k in range(zz):
                for h in range(PARTS):
                    w_copy(k, q, h).wait_recv()
                    if zz < last:
                        send(w_copy(k, q, h))
                acc[zz, q] = acc[zz, q] - jnp.dot(
                    ufull[:, k * BLK:(k + 1) * BLK], w[k, q], preferred_element_type=F32)
            w[zz, q] = acc[zz, q].astype(BF)
            if zz < last:
                for h in range(PARTS):
                    send(w_copy(zz, q, h))
            send(out_copy(q))
            own_copy(q).start()
            if zz == 0 and q + 1 < chunks:
                for k in range(1, last):
                    for h in range(PARTS):
                        up_copy(k, q + 1, h).start()
        for copy in sent:
            copy.wait_send()
        for q in range(chunks):
            for h in range(PARTS):
                if zz == 0:
                    for k in range(1, chips):
                        up_copy(k, q, h).wait_send()
                if zz == last:
                    for k in range(last):
                        dn_copy(k, q, h).wait_send()

    for zz in range(chips):
        pl.when(z == zz)(functools.partial(role, zz))

    for q in range(chunks):
        own_copy(q).wait()
        out_copy(q).wait_recv()
    for k in range(chips):
        sib_copy(k).wait_send()
    xd.wait_send()
    xu.wait_send()


def fused_call(dosages, allele_freq, earlier_factor, earlier_solved, diag_inverse, update_products):
    slab = earlier_factor.shape[0]
    chips = slab // BLK
    snps = dosages.shape[0]
    width = earlier_solved.shape[1]
    half = width // 2
    chunks = half // CW
    rows = diag_inverse.shape[0]
    depth = earlier_factor.shape[1]
    pieces = (chips, chunks, BLK, CW)
    dma = pltpu.SemaphoreType.DMA
    hbm = pl.BlockSpec(memory_space=pl.ANY)
    vmem = pl.BlockSpec(memory_space=pltpu.VMEM)
    macs = slab * depth * width + rows * (BLK + slab) * width
    return pl.pallas_call(
        functools.partial(fused, chips),
        out_shape=jax.ShapeDtypeStruct((rows, width), BF),
        in_specs=[hbm, vmem, hbm, hbm, hbm, hbm],
        out_specs=hbm,
        scratch_shapes=[
            pltpu.VMEM((snps, slab), jnp.int32),
            pltpu.VMEM((slab, depth), BF),
            pltpu.VMEM((depth, width), BF),
            pltpu.VMEM((BLK, BLK), BF),
            pltpu.VMEM((BLK, slab - BLK), BF),
            pltpu.VMEM((slab, half), BF),
            pltpu.VMEM(pieces, F32),
            pltpu.VMEM((chips, BLK, half), BF),
            pltpu.VMEM((chips, BLK, half), BF),
            pltpu.VMEM(pieces, BF),
            pltpu.VMEM(pieces, BF),
            pltpu.VMEM(pieces, BF),
            pltpu.VMEM(pieces, BF),
            pltpu.VMEM(pieces, BF),
            dma((4,)), dma((chips,)), dma((4,)), dma((chips,)), dma((chips,)),
            *[dma((chips, chunks * PARTS))] * 6,
            dma((chunks,)), dma((chunks,)), dma((chunks,)),
        ],
        compiler_params=pltpu.CompilerParams(
            collective_id=0, has_side_effects=True, vmem_limit_bytes=60 * 2**20),
        cost_estimate=pl.CostEstimate(
            flops=2 * macs, bytes_accessed=8 * 2**20, transcendentals=0),
    )(dosages, allele_freq.reshape(1, snps), earlier_factor, earlier_solved,
      diag_inverse, update_products)


def exchange_2(value, axis, stride):
    mask = 2**stride
    pairs = [(source, source ^ mask) for source in range(lax.axis_size(axis))]
    return lax.ppermute(value, axis, pairs)


def general(dosages, allele_freq, earlier_factor, earlier_solved, diag_inverse, update_products):
    slab = earlier_factor.shape[0]
    frequency = allele_freq[:, None]
    scaled = (
        (dosages.astype(F32) - 2.0 * frequency)
        * lax.rsqrt(2.0 * frequency * (1.0 - frequency))
    ).astype(BF)
    arrived = lax.all_to_all(scaled, "ind", split_axis=1, concat_axis=0, tiled=True)
    rows_dev = diag_inverse.shape[0]
    update = lax.psum_scatter(
        jnp.dot(earlier_factor, earlier_solved, preferred_element_type=F32),
        "ind", scatter_dimension=0, tiled=True)
    residual = (arrived.T.astype(F32) - update).astype(BF)
    position = lax.axis_index("ind")
    my_block = position * rows_dev // BLK
    held = residual
    for bit in range((BLK // rows_dev).bit_length() - 1):
        other = exchange_2(held, "ind", bit)
        held = jnp.where(
            position // 2**bit % 2 == 0,
            jnp.concatenate((held, other), 0), jnp.concatenate((other, held), 0))
    diagonal_term = jnp.dot(diag_inverse, held, preferred_element_type=F32)
    solved = jnp.where(my_block == 0, diagonal_term.astype(BF), jnp.zeros_like(residual))
    for block in range(1, slab // BLK):
        carried = jnp.dot(
            update_products, lax.all_gather(solved, "ind", axis=0, tiled=True),
            preferred_element_type=F32)
        solved = jnp.where(my_block == block, (diagonal_term - carried).astype(BF), solved)
    return solved


def solution(mesh):
    def per_device(*args):
        slab = args[2].shape[0]
        if mesh.shape["ind"] * BLK == 2 * slab and args[3].shape[1] % (2 * CW) == 0:
            return fused_call(*args)
        return general(*args)

    placed = (
        P(("snp", "ind"), None),
        P(("snp", "ind")),
        P(None, "ind"),
        P("ind", "snp"),
        P("ind", None),
        P("ind", None),
    )
    return jax.shard_map(
        per_device, mesh=mesh, in_specs=placed, out_specs=P("ind", "snp"), check_vma=False
    )
```

```python
import functools
import jax
import jax.numpy as jnp
from jax import lax
from jax.experimental import pallas as pl
from jax.experimental.pallas import tpu as pltpu
from jax.sharding import PartitionSpec as P

BLK = 512
CW = 128
PR = 256
PARTS = BLK // PR
BF = jnp.bfloat16
F32 = jnp.float32


def fused(chips, dos_h, freq_ref, a_h, b_h, d_h, u_h, out_ref,
          dos, a, b, dfull, ufull, placed, acc, sib_out, sib_in,
          up_out, up_in, dn_out, dn_in, w,
          ld_sem, a_sem, x_sem, sib_s, sib_r, up_s, up_r, dn_s, dn_r, w_s, w_r, o_s, o_r, l_s):
    me = lax.axis_index("ind")
    z, c = me // 2, me % 2
    sib = z * 2 + 1 - c
    half = b_h.shape[1] // 2
    chunks = half // CW
    rows = d_h.shape[0]
    ucols = ufull.shape[1]
    snps = dos_h.shape[0]

    def remote(src, dst, ss, rs, to):
        return pltpu.make_async_remote_copy(
            src_ref=src, dst_ref=dst, send_sem=ss, recv_sem=rs,
            device_id={"ind": to}, device_id_type=pl.DeviceIdType.MESH)

    last = chips - 1

    def block_at(j):
        bottom = jnp.where(j == 0, last, jnp.where(j == last, 0, j))
        return jnp.where(z == 0, bottom, lax.rem(z + 1 + j, chips))

    def load_a(j):
        at = pl.ds(pl.multiple_of(block_at(j) * BLK, BLK), BLK)
        return pltpu.make_async_copy(a_h.at[at], a.at[at], a_sem.at[j])

    my_rows = pl.ds(pl.multiple_of(c * rows, rows), rows)
    load_dos = pltpu.make_async_copy(dos_h, dos, ld_sem.at[0])
    load_b = pltpu.make_async_copy(b_h, b, ld_sem.at[1])
    load_d = pltpu.make_async_copy(d_h, dfull.at[my_rows], ld_sem.at[2])
    load_u = pltpu.make_async_copy(u_h.at[:, :ucols], ufull.at[my_rows], ld_sem.at[3])
    load_dos.start()
    load_b.start()
    for j in range(chips):
        load_a(j).start()
    load_d.start()
    load_u.start()

    barrier = pltpu.get_barrier_semaphore()

    def greet(to):
        pl.semaphore_signal(barrier, inc=1, device_id={"ind": to},
                            device_id_type=pl.DeviceIdType.MESH)

    greet(sib)

    @pl.when(z > 0)
    def _():
        greet(me - 2)

    @pl.when(z < chips - 1)
    def _():
        greet(me + 2)

    load_dos.wait()
    frow = freq_ref[...]
    eye = (lax.broadcasted_iota(jnp.int32, (snps, snps), 0)
           == lax.broadcasted_iota(jnp.int32, (snps, snps), 1))
    freq = jnp.sum(jnp.where(eye, jnp.broadcast_to(frow, (snps, snps)), 0.0), axis=1, keepdims=True)
    scaled = ((dos[...].astype(F32) - 2.0 * freq)
              * lax.rsqrt(2.0 * freq * (1.0 - freq))).astype(BF)
    my_side = me * snps // half
    place = (lax.broadcasted_iota(jnp.int32, (snps, half), 1) + my_side * half
             == lax.broadcasted_iota(jnp.int32, (snps, half), 0) + me * snps)
    placed[...] = lax.dot_general(scaled, place.astype(F32).astype(BF), (((0,), (0,)), ((), ())),
                                  preferred_element_type=F32).astype(BF)

    @pl.when((z == 0) | (z == chips - 1))
    def _():
        pl.semaphore_wait(barrier, 2)

    @pl.when((z > 0) & (z < chips - 1))
    def _():
        pl.semaphore_wait(barrier, 3)

    xd = remote(d_h, dfull.at[my_rows], x_sem.at[0], x_sem.at[1], sib)
    xu = remote(u_h.at[:, :ucols], ufull.at[my_rows], x_sem.at[2], x_sem.at[3], sib)

    def sib_copy(blk):
        return remote(sib_out.at[blk], sib_in.at[blk], sib_s.at[blk], sib_r.at[blk], sib)

    def piece(buf, blk, q, h):
        return buf.at[blk, q, pl.ds(h * PR, PR)]

    def line_copy(src, dst, ss, rs, blk, q, h, to):
        return remote(piece(src, blk, q, h), piece(dst, blk, q, h),
                      ss.at[blk, q * PARTS + h], rs.at[blk, q * PARTS + h], to)

    def up_copy(blk, q, h):
        return line_copy(up_out, up_in, up_s, up_r, blk, q, h, me + 2)

    def dn_copy(blk, q, h):
        return line_copy(dn_out, dn_in, dn_s, dn_r, blk, q, h, me - 2)

    def w_copy(blk, q, h):
        return line_copy(w, w, w_s, w_r, blk, q, h, me + 2)

    def out_copy(q):
        return remote(
            w.at[z, q, pl.ds(pl.multiple_of((1 - c) * rows, rows), rows)],
            out_ref.at[:, pl.ds(pl.multiple_of(c * half + q * CW, CW), CW)],
            o_s.at[q], o_r.at[q], sib)

    def own_copy(q):
        return pltpu.make_async_copy(
            w.at[z, q, my_rows],
            out_ref.at[:, pl.ds(pl.multiple_of(c * half + q * CW, CW), CW)], l_s.at[q])

    def partial(blk, side):
        at = pl.ds(pl.multiple_of(blk * BLK, BLK), BLK)
        cols = pl.ds(pl.multiple_of(side * half, half), half)
        own = jnp.where(side == my_side, placed[at, :].astype(F32), 0.0)
        return own - jnp.dot(a[at, :], b[:, cols], preferred_element_type=F32)

    def finish(blk):
        sib_copy(blk).wait_recv()
        for q in range(chunks):
            total = acc[blk, q] + sib_in[blk, :, q * CW:(q + 1) * CW].astype(F32)
            acc[blk, q] = total

            @pl.when((z == 0) & (blk > 0))
            def _():
                up_out[blk, q] = total.astype(BF)

            @pl.when((z == 0) & (blk > (last - 1 if q else 0)))
            def _():
                for h in range(PARTS):
                    up_copy(blk, q, h).start()

            @pl.when((z == last) & (blk < last))
            def _():
                dn_out[blk, q] = total.astype(BF)
                for h in range(PARTS):
                    dn_copy(blk, q, h).start()

    load_b.wait()

    def step(j, carry):
        load_a(j).wait()
        blk = block_at(j)
        sib_out[blk] = partial(blk, 1 - c).astype(BF)
        sib_copy(blk).start()
        own = partial(blk, c)
        for q in range(chunks):
            acc[blk, q] = own[:, q * CW:(q + 1) * CW]

        @pl.when(j > 0)
        def _():
            finish(block_at(j - 1))

        return carry

    lax.fori_loop(0, chips, step, 0)
    xd.start()
    xu.start()
    finish(block_at(chips - 1))

    def role(zz):
        sent = []

        def send(copy):
            copy.start()
            sent.append(copy)

        def relay(copy, out, arrived, blk, q):
            for h in range(PARTS):
                at = slice(h * PR, (h + 1) * PR)
                copy(blk, q, h).wait_recv()
                out[blk, q, at] = (acc[blk, q, at] + arrived[blk, q, at].astype(F32)).astype(BF)
                send(copy(blk, q, h))

        def relay_up(blk, q):
            relay(up_copy, up_out, up_in, blk, q)

        def relay_dn(blk, q):
            relay(dn_copy, dn_out, dn_in, blk, q)

        def residual(q):
            total = acc[zz, q]
            if zz < last:
                for h in range(PARTS):
                    dn_copy(zz, q, h).wait_recv()
                total = total + dn_in[zz, q].astype(F32)
            if zz > 0:
                for h in range(PARTS):
                    up_copy(zz, q, h).wait_recv()
                total = total + up_in[zz, q].astype(F32)
            acc[zz, q] = jnp.dot(dfull[...], total.astype(BF), preferred_element_type=F32)

        ready = []

        def weights():
            if not ready:
                load_d.wait()
                load_u.wait()
                xd.wait_recv()
                xu.wait_recv()
                ready.append(1)

        if 0 < zz < last:
            pieces = [(2 * k + last - zz + q - 0.6, q, 0, k) for k in range(zz) for q in range(chunks)]
            pieces += [(zz + q, q, 1, last) for q in range(chunks)]
            pieces += [(zz + 1 + k, 0, 1, k) for k in range(zz + 1, last)]
            for _, q, up, k in sorted(pieces):
                (relay_up if up else relay_dn)(k, q)
        weights()
        for q in range(chunks):
            if q:
                for k in range(zz + 1, last):
                    if zz > 0:
                        relay_up(k, q)
            residual(q)
            for k in range(zz):
                for h in range(PARTS):
                    w_copy(k, q, h).wait_recv()
                    if zz < last:
                        send(w_copy(k, q, h))
                acc[zz, q] = acc[zz, q] - jnp.dot(
                    ufull[:, k * BLK:(k + 1) * BLK], w[k, q], preferred_element_type=F32)
            w[zz, q] = acc[zz, q].astype(BF)
            if zz < last:
                for h in range(PARTS):
                    send(w_copy(zz, q, h))
            send(out_copy(q))
            own_copy(q).start()
            if zz == 0 and q + 1 < chunks:
                for k in range(1, last):
                    for h in range(PARTS):
                        up_copy(k, q + 1, h).start()
        for copy in sent:
            copy.wait_send()
        for q in range(chunks):
            for h in range(PARTS):
                if zz == 0:
                    for k in range(1, chips):
                        up_copy(k, q, h).wait_send()
                if zz == last:
                    for k in range(last):
                        dn_copy(k, q, h).wait_send()

    for zz in range(chips):
        pl.when(z == zz)(functools.partial(role, zz))

    for q in range(chunks):
        own_copy(q).wait()
        out_copy(q).wait_recv()
    for k in range(chips):
        sib_copy(k).wait_send()
    xd.wait_send()
    xu.wait_send()


def fused_call(dosages, allele_freq, earlier_factor, earlier_solved, diag_inverse, update_products):
    slab = earlier_factor.shape[0]
    chips = slab // BLK
    snps = dosages.shape[0]
    width = earlier_solved.shape[1]
    half = width // 2
    chunks = half // CW
    rows = diag_inverse.shape[0]
    depth = earlier_factor.shape[1]
    pieces = (chips, chunks, BLK, CW)
    dma = pltpu.SemaphoreType.DMA
    hbm = pl.BlockSpec(memory_space=pl.ANY)
    vmem = pl.BlockSpec(memory_space=pltpu.VMEM)
    macs = slab * depth * width + rows * (BLK + slab) * width
    return pl.pallas_call(
        functools.partial(fused, chips),
        out_shape=jax.ShapeDtypeStruct((rows, width), BF),
        in_specs=[hbm, vmem, hbm, hbm, hbm, hbm],
        out_specs=hbm,
        scratch_shapes=[
            pltpu.VMEM((snps, slab), jnp.int32),
            pltpu.VMEM((slab, depth), BF),
            pltpu.VMEM((depth, width), BF),
            pltpu.VMEM((BLK, BLK), BF),
            pltpu.VMEM((BLK, slab - BLK), BF),
            pltpu.VMEM((slab, half), BF),
            pltpu.VMEM(pieces, F32),
            pltpu.VMEM((chips, BLK, half), BF),
            pltpu.VMEM((chips, BLK, half), BF),
            pltpu.VMEM(pieces, BF),
            pltpu.VMEM(pieces, BF),
            pltpu.VMEM(pieces, BF),
            pltpu.VMEM(pieces, BF),
            pltpu.VMEM(pieces, BF),
            dma((4,)), dma((chips,)), dma((4,)), dma((chips,)), dma((chips,)),
            *[dma((chips, chunks * PARTS))] * 6,
            dma((chunks,)), dma((chunks,)), dma((chunks,)),
        ],
        compiler_params=pltpu.CompilerParams(
            collective_id=0, has_side_effects=True, vmem_limit_bytes=60 * 2**20),
        cost_estimate=pl.CostEstimate(
            flops=2 * macs, bytes_accessed=8 * 2**20, transcendentals=0),
    )(dosages, allele_freq.reshape(1, snps), earlier_factor, earlier_solved,
      diag_inverse, update_products)


def exchange_2(value, axis, stride):
    mask = 2**stride
    pairs = [(source, source ^ mask) for source in range(lax.axis_size(axis))]
    return lax.ppermute(value, axis, pairs)


def general(dosages, allele_freq, earlier_factor, earlier_solved, diag_inverse, update_products):
    slab = earlier_factor.shape[0]
    frequency = allele_freq[:, None]
    scaled = (
        (dosages.astype(F32) - 2.0 * frequency)
        * lax.rsqrt(2.0 * frequency * (1.0 - frequency))
    ).astype(BF)
    arrived = lax.all_to_all(scaled, "ind", split_axis=1, concat_axis=0, tiled=True)
    rows_dev = diag_inverse.shape[0]
    update = lax.psum_scatter(
        jnp.dot(earlier_factor, earlier_solved, preferred_element_type=F32),
        "ind", scatter_dimension=0, tiled=True)
    residual = (arrived.T.astype(F32) - update).astype(BF)
    position = lax.axis_index("ind")
    my_block = position * rows_dev // BLK
    held = residual
    for bit in range((BLK // rows_dev).bit_length() - 1):
        other = exchange_2(held, "ind", bit)
        held = jnp.where(
            position // 2**bit % 2 == 0,
            jnp.concatenate((held, other), 0), jnp.concatenate((other, held), 0))
    diagonal_term = jnp.dot(diag_inverse, held, preferred_element_type=F32)
    solved = jnp.where(my_block == 0, diagonal_term.astype(BF), jnp.zeros_like(residual))
    for block in range(1, slab // BLK):
        carried = jnp.dot(
            update_products, lax.all_gather(solved, "ind", axis=0, tiled=True),
            preferred_element_type=F32)
        solved = jnp.where(my_block == block, (diagonal_term - carried).astype(BF), solved)
    return solved


def solution(mesh):
    def per_device(*args):
        slab = args[2].shape[0]
        if mesh.shape["ind"] * BLK == 2 * slab and args[3].shape[1] % (2 * CW) == 0:
            return fused_call(*args)
        return general(*args)

    placed = (
        P(("snp", "ind"), None),
        P(("snp", "ind")),
        P(None, "ind"),
        P("ind", "snp"),
        P("ind", None),
        P("ind", None),
    )
    return jax.shard_map(
        per_device, mesh=mesh, in_specs=placed, out_specs=P("ind", "snp"), check_vma=False
    )
```
